32 devices in a mesh: dp: 8 (over z, y), mp: 4 (over x, core).
Axes of the slice: x: 2, y: 2, z: 4, core: 2. Of those that a mesh axis runs over, the one named last changes fastest.
Arguments:
- tokens: bfloat16 [14336, 1024], P('dp'), may hold values from -60 to 60
- segment_ids: int32 [14336], P('dp'), may hold values from 0 to 31, as said below
- page_table: int32 [112], P('dp'), may hold values from 0 to 111, as said below
- w_query: bfloat16 [1024, 1024], P('dp', 'mp'), may hold values from -0.1875 to 0.1875
- w_key: bfloat16 [1024, 1024], P('dp', 'mp'), may hold values from -0.1875 to 0.1875
- w_value: bfloat16 [1024, 1024], P('dp', 'mp'), may hold values from -0.1875 to 0.1875
- w_out: bfloat16 [1024, 1024], P('mp', 'dp'), may hold values from -1.5 to 1.5
- w_up: bfloat16 [1024, 4096], P('dp', 'mp'), may hold values from -0.1875 to 0.1875
- w_down: bfloat16 [4096, 1024], P('mp', 'dp'), may hold values from -0.09375 to 0.09375
- gain_first: float32 [1024], replicated, may hold values from 0.1 to 1.9
- shift_first: float32 [1024], replicated, may hold values from -3 to 3
- gain_second: float32 [1024], replicated, may hold values from 0.1 to 1.9
- shift_second: float32 [1024], replicated, may hold values from -3 to 3
Outputs:
- mixed: bfloat16 [14336, 1024], P('dp')
- kv_cache: bfloat16 [14336, 2, 1024], P('dp', None, 'mp')
The draws below stay inside these ranges and needn't reach their ends.
Inputs may be any that keep to these rules, and one draw needn't show every extreme that they name: page_table is a permutation of the page slots. Page p lies on device p // 14 in arrival order and goes to device page_table[p] // 14; from one device at most 2 pages go to one device, and some pair reaches 2. `segment_ids`: tokens with equal ids form one request; after dealing, a request's tokens are consecutive and lie on one device, which holds at most 4 requests.
All inputs are finite; a program needn't handle non-finite values.
Results may differ from the reference program's by a relative error of at most 0.014.
Values may be sent and summed in bfloat16 or wider, within the bound.
A program may use at most 128 MiB of HBM per device.

```python
import jax
import jax.numpy as jnp
from jax import lax

D = 1024
HEADS = 16
HEAD = 64
FF = 4096
PAGE = 128
PAGES_DEV = 14
REQS_DEV = 4
TOK_DEV = 1792
TOKENS = 14336
NPAGES = 112
N_DP = 8
N_MP = 4


def dealing(key):
    key_table = jax.random.fold_in(key, 11)
    key_slots = jax.random.fold_in(key, 12)
    key_cuts = jax.random.fold_in(key, 13)
    shuffled = jax.random.permutation(key_table, N_DP).astype(jnp.int32)
    every = jnp.arange(N_DP, dtype=jnp.int32)
    marked = (every == N_DP // 2) | (every == 1) | (every == N_DP - 1)
    score = shuffled + N_DP * marked.astype(jnp.int32)
    offsets = jnp.argsort(-score).astype(jnp.int32)
    page_index = jnp.arange(PAGES_DEV, dtype=jnp.int32)
    sources = jnp.arange(N_DP, dtype=jnp.int32)
    target = (sources[:, None] + offsets[page_index % N_DP][None, :]) % N_DP
    orders = jax.vmap(lambda sub_key: jax.random.permutation(sub_key, PAGES_DEV).astype(jnp.int32))(jax.random.split(key_slots, N_DP))
    slots = orders[target, jnp.broadcast_to(page_index[None, :], target.shape)]
    table = (target * PAGES_DEV + slots).reshape(-1).astype(jnp.int32)
    cuts = jnp.sort(jax.random.randint(key_cuts, (N_DP, REQS_DEV - 1), 1, TOK_DEV), axis=1)
    position = jnp.arange(TOK_DEV, dtype=jnp.int32)
    counts = jnp.sum((cuts[:, None, :] <= position[None, :, None]).astype(jnp.int32), axis=2)
    dealt_ids = (sources[:, None] * REQS_DEV + counts).reshape(NPAGES, PAGE)
    arrival_ids = dealt_ids[table].reshape(-1).astype(jnp.int32)
    return (table, arrival_ids)


def draw_page_table(key, part):
    return dealing(key)[0]


def draw_segment_ids(key, part):
    return dealing(key)[1]


def draw_tokens(key, part):
    key_base = jax.random.fold_in(key, 1)
    base = jax.random.normal(key_base, (TOKENS, D), jnp.float32)
    return jnp.clip(base, -60.0, 60.0).astype(jnp.bfloat16)


def level_of(own_key, dims, pieces, least, top_value):
    level, own = 1.0, jax.random.fold_in(own_key, 6)
    for axis_at, parts in pieces:
        steps = jnp.exp(jax.random.uniform(jax.random.fold_in(own, axis_at), (parts,), jnp.float32, least / len(pieces), top_value / len(pieces)))
        level = level * jnp.repeat(steps, dims[axis_at] // parts).reshape([-1 if axis == axis_at else 1 for axis in range(len(dims))])
    return level


def noise(own_key, extent, deviation, limit, cuts=(), held_as=jnp.bfloat16):
    entries = jax.random.normal(own_key, extent, jnp.float32) * deviation
    if len(cuts) > 0:
        entries = level_of(own_key, extent, cuts, -0.22, 0.18) * entries
    return jnp.clip(entries, min=-limit, max=limit).astype(held_as)


def setup_inputs(seed: int = 0) -> dict:
    arg_keys = jax.random.split(jax.random.key(seed), 14)
    tokens = draw_tokens(jax.random.fold_in(arg_keys[13], 71), 0)
    segment_ids = draw_segment_ids(jax.random.fold_in(arg_keys[13], 71), 0)
    page_table = draw_page_table(jax.random.fold_in(arg_keys[13], 71), 0)
    w_query = noise(arg_keys[3], (D, D), D ** -0.5, 0.1875, ((0, 8), (1, 4)))
    w_key = noise(arg_keys[4], (D, D), D ** -0.5, 0.1875, ((0, 8), (1, 4)))
    w_value = noise(arg_keys[5], (D, D), D ** -0.5, 0.1875, ((0, 8), (1, 4)))
    w_out = noise(arg_keys[6], (D, D), (HEAD // 4) ** -0.5, 1.5, ((0, 4), (1, 8)))
    w_up = noise(arg_keys[7], (D, FF), D ** -0.5, 0.1875, ((0, 8), (1, 4)))
    w_down = noise(arg_keys[8], (FF, D), FF ** -0.5, 0.09375, ((0, 4), (1, 8)))
    gain_first = jnp.clip(1.0 + 0.18 * jax.random.normal(arg_keys[9], (D,), jnp.float32), 0.1, 1.9)
    shift_first = noise(arg_keys[10], (D,), 0.5, 3.0, (), jnp.float32)
    gain_second = jnp.clip(1.0 + 0.18 * jax.random.normal(arg_keys[11], (D,), jnp.float32), 0.1, 1.9)
    shift_second = noise(arg_keys[12], (D,), 0.5, 3.0, (), jnp.float32)
    return dict(tokens=tokens, segment_ids=segment_ids, page_table=page_table, w_query=w_query, w_key=w_key, w_value=w_value, w_out=w_out, w_up=w_up, w_down=w_down, gain_first=gain_first, shift_first=shift_first, gain_second=gain_second, shift_second=shift_second)


def layer_norm(hidden_sum, gain, shift):
    center = hidden_sum - lax.optimization_barrier(jnp.mean(hidden_sum, axis=-1, keepdims=True))
    spread = lax.optimization_barrier(jnp.mean(center * center, axis=-1, keepdims=True))
    return center * lax.rsqrt(spread + 1e-05) * gain + shift

def attend_head(query, keys, values, segments):
    scores = jnp.einsum('qd,kd->qk', query.astype(jnp.float32), keys.astype(jnp.float32)) * HEAD ** (-0.5)
    scores = jnp.where(segments[:, None] == segments[None, :], scores, -1e+30)
    highest = lax.optimization_barrier(jnp.max(scores, axis=1, keepdims=True))
    raised = jnp.exp(scores - highest)
    attn_weights = (raised / lax.optimization_barrier(jnp.sum(raised, axis=1, keepdims=True))).astype(jnp.bfloat16)
    return jnp.dot(attn_weights, values, preferred_element_type=jnp.float32).astype(jnp.bfloat16)

def reference(tokens, segment_ids, page_table, w_query, w_key, w_value, w_out, w_up, w_down, gain_first, shift_first, gain_second, shift_second):
    pages = tokens.reshape(NPAGES, PAGE, D)
    dealt = jnp.zeros_like(pages).at[page_table].set(pages).reshape(N_DP, TOK_DEV, D)
    dealt_ids = jnp.zeros((NPAGES, PAGE), jnp.int32).at[page_table].set(segment_ids.reshape(NPAGES, PAGE)).reshape(N_DP, TOK_DEV)
    group_heads = HEADS // N_MP
    group_width = D // N_MP
    group_units = FF // N_MP

    def device_layer(bundle):
        rows, segments = bundle
        query = jnp.dot(rows, w_query, preferred_element_type=jnp.float32).astype(jnp.bfloat16)
        keys = jnp.dot(rows, w_key, preferred_element_type=jnp.float32).astype(jnp.bfloat16)
        values = jnp.dot(rows, w_value, preferred_element_type=jnp.float32).astype(jnp.bfloat16)
        attended = jnp.zeros((TOK_DEV, D), jnp.float32)
        for group in range(N_MP):
            heads = []
            for head in range(group * group_heads, (group + 1) * group_heads):
                cols = slice(head * HEAD, (head + 1) * HEAD)
                heads.append(attend_head(query[:, cols], keys[:, cols], values[:, cols], segments))
            context = jnp.concatenate(heads, axis=1)
            term = jnp.dot(context, w_out[group * group_width:(group + 1) * group_width], preferred_element_type=jnp.float32).astype(jnp.bfloat16)
            attended = attended + lax.optimization_barrier(term).astype(jnp.float32)
        first = layer_norm(rows.astype(jnp.float32) + attended, gain_first, shift_first).astype(jnp.bfloat16)
        fed = jnp.zeros((TOK_DEV, D), jnp.float32)
        for group in range(N_MP):
            units = slice(group * group_units, (group + 1) * group_units)
            hidden = jax.nn.gelu(jnp.dot(first, w_up[:, units], preferred_element_type=jnp.float32), approximate=False).astype(jnp.bfloat16)
            term = jnp.dot(hidden, w_down[units], preferred_element_type=jnp.float32).astype(jnp.bfloat16)
            fed = fed + lax.optimization_barrier(term).astype(jnp.float32)
        second = layer_norm(first.astype(jnp.float32) + fed, gain_second, shift_second).astype(jnp.bfloat16)
        return (second, jnp.stack([keys, values], axis=1))
    second, cache = lax.map(device_layer, (dealt, dealt_ids))
    mixed = second.reshape(NPAGES, PAGE, D)[page_table].reshape(TOKENS, D)
    return (mixed, cache.reshape(TOKENS, 2, D))
```

```python
import functools

import jax
import jax.numpy as jnp
from jax import lax
from jax.experimental import pallas as pl
from jax.experimental.pallas import tpu as pltpu
from jax.sharding import PartitionSpec as P

HEAD = 64
MESH = pl.DeviceIdType.MESH
VMEM_BYTES = 48 * 1024 * 1024


def mp_peers(me_m, n_mp):
    return me_m + 1 - 2 * lax.rem(me_m, 2), lax.rem(me_m + 2, n_mp)


def swap_kernel(n_dp, n_mp, with_extra, *refs):
    if with_extra:
        send, meta, weight, recv, got_meta, full, *sems = refs
    else:
        send, recv, *sems = refs
    local, a_send, a_recv, f_send, f_recv, *more = sems
    me_d, me_m = lax.axis_index("dp"), lax.axis_index("mp")
    sib, far = mp_peers(me_m, n_mp)
    barrier = pltpu.get_barrier_semaphore()
    for k in range(1, n_dp):
        pl.semaphore_signal(
            barrier, inc=1, device_id=(lax.rem(me_d + k, n_dp), me_m), device_id_type=MESH
        )
    for peer in (sib, far):
        pl.semaphore_signal(barrier, inc=1, device_id=(me_d, peer), device_id_type=MESH)
    pl.semaphore_wait(barrier, n_dp + 1)

    def remote(src, dst, s_sem, r_sem, dev):
        return pltpu.make_async_remote_copy(
            src_ref=src,
            dst_ref=dst,
            send_sem=s_sem,
            recv_sem=r_sem,
            device_id=dev,
            device_id_type=MESH,
        )

    def source(k):
        return lax.rem(me_d - k + n_dp, n_dp)

    own = pltpu.make_async_copy(send.at[me_d], recv.at[me_d, :, me_m], local.at[0])
    own.start()
    outs = []
    if with_extra:
        m_send, m_recv, z_send, z_recv, y_send, y_recv = more
        own_meta = pltpu.make_async_copy(meta.at[me_d], got_meta.at[me_d], local.at[1])
        own_meta.start()
        own_w = pltpu.make_async_copy(weight, full.at[me_d], local.at[2])
        own_w.start()
        for k in range(1, n_dp):
            to = lax.rem(me_d + k, n_dp)
            outs.append(
                remote(meta.at[to], got_meta.at[me_d], m_send.at[k], m_recv.at[k], (to, me_m))
            )
            outs[-1].start()
    for k in range(1, n_dp):
        to = lax.rem(me_d + k, n_dp)
        outs.append(
            remote(send.at[to], recv.at[me_d, :, me_m], a_send.at[k], a_recv.at[k], (to, me_m))
        )
        outs[-1].start()
    if with_extra:
        rows = n_dp // 2
        b = lax.rem(me_d, 2)
        a = (me_d - b) // 2
        across = me_d + 1 - 2 * b
        outs.append(remote(weight, full.at[me_d], y_send.at[0], y_recv.at[0], (me_d + 1 - 2 * b, me_m)))
        outs[-1].start()
        for k in range(1, rows):
            to = lax.rem(a + k, rows) * 2 + b
            outs.append(remote(weight, full.at[me_d], z_send.at[k], z_recv.at[k], (to, me_m)))
            outs[-1].start()

    def hand_on(k):
        block = recv.at[source(k), :, me_m]
        for way, peer in ((0, far), (1, sib)):
            outs.append(
                remote(block, block, f_send.at[way, k], f_recv.at[way, k], (me_d, peer))
            )
            outs[-1].start()

    def hand_far(k):
        block = recv.at[source(k), :, far]
        remote(block, block, f_send.at[0, k], f_recv.at[0, k], (me_d, far)).wait_recv()
        outs.append(remote(block, block, f_send.at[2, k], f_recv.at[2, k], (me_d, sib)))
        outs[-1].start()

    own.wait()
    hand_on(0)
    for k in range(1, n_dp):
        block = recv.at[source(k), :, me_m]
        remote(block, block, a_send.at[k], a_recv.at[k], (me_d, far)).wait_recv()
        hand_on(k)
        hand_far(k - 1)
    hand_far(n_dp - 1)
    if with_extra:
        for k in range(1, rows):
            block = full.at[lax.rem(a - k + rows, rows) * 2 + b]
            remote(block, block, z_send.at[k], z_recv.at[k], (across, me_m)).wait_recv()
            outs.append(remote(block, block, y_send.at[k], y_recv.at[k], (across, me_m)))
            outs[-1].start()
        for k in range(rows):
            block = full.at[lax.rem(a - k + rows, rows) * 2 + 1 - b]
            remote(block, block, y_send.at[k], y_recv.at[k], (across, me_m)).wait_recv()
        for k in range(1, n_dp):
            block = got_meta.at[source(k)]
            remote(block, block, m_send.at[k], m_recv.at[k], (across, me_m)).wait_recv()
        own_meta.wait()
        own_w.wait()
    sib_far = lax.rem(sib + 2, n_mp)
    for k in range(n_dp):
        for way, quarter in ((1, sib), (2, sib_far)):
            block = recv.at[source(k), :, quarter]
            remote(block, block, f_send.at[way, k], f_recv.at[way, k], (me_d, sib)).wait_recv()
    for copy in outs:
        copy.wait_send()


def swap(send, n_mp, collective_id, meta=None, weight=None):
    n_dp, slots, rows, width = send.shape
    with_extra = meta is not None
    any_spec = pl.BlockSpec(memory_space=pl.ANY)
    outs = [jax.ShapeDtypeStruct((n_dp, slots, n_mp, rows, width), send.dtype)]
    sems = [(3,), (n_dp,), (n_dp,), (3, n_dp), (3, n_dp)]
    args = [send]
    if with_extra:
        outs += [
            jax.ShapeDtypeStruct(meta.shape, meta.dtype),
            jax.ShapeDtypeStruct((n_dp, *weight.shape), weight.dtype),
        ]
        sems += [(n_dp,), (n_dp,)] + [(n_dp // 2,)] * 4
        args += [meta, weight]
    return pl.pallas_call(
        functools.partial(swap_kernel, n_dp, n_mp, with_extra),
        out_shape=outs,
        in_specs=[any_spec] * len(args),
        out_specs=[any_spec] * len(outs),
        scratch_shapes=[pltpu.SemaphoreType.DMA(s) for s in sems],
        compiler_params=pltpu.CompilerParams(collective_id=collective_id, has_side_effects=True),
        name=f"swap_{collective_id}",
    )(*args)


def reduce_kernel(n_mp, chunk, gather, *refs):
    part, resid, gain, shift, out, sib_in, acc, far_in, res, *sems = refs
    local, s_send, s_recv, x_send, x_recv, *more = sems
    me_d, me_m = lax.axis_index("dp"), lax.axis_index("mp")
    sib, far = mp_peers(me_m, n_mp)
    sib_far = lax.rem(sib + 2, n_mp)
    chunks = part.shape[0] // chunk
    barrier = pltpu.get_barrier_semaphore()
    for peer in (sib, far):
        pl.semaphore_signal(barrier, inc=1, device_id=(me_d, peer), device_id_type=MESH)
    pl.semaphore_wait(barrier, 2)
    if gather:
        own = pltpu.make_async_copy(resid.at[:, me_m], res, local.at[0])
    else:
        own = pltpu.make_async_copy(resid.at[:, me_m], res, local.at[0])
    own.start()

    def at(c):
        return pl.ds(c * chunk, chunk)

    def to_sib(half, c):
        quarter = sib_far if half == 0 else sib
        return pltpu.make_async_remote_copy(
            src_ref=part.at[at(c), quarter],
            dst_ref=sib_in.at[half, at(c)],
            send_sem=s_send.at[half, c],
            recv_sem=s_recv.at[half, c],
            device_id=(me_d, sib),
            device_id_type=MESH,
        )

    def to_far(c):
        return pltpu.make_async_remote_copy(
            src_ref=acc.at[at(c)],
            dst_ref=far_in.at[at(c)],
            send_sem=x_send.at[c],
            recv_sem=x_recv.at[c],
            device_id=(me_d, far),
            device_id_type=MESH,
        )

    def spread(way, c, quarter):
        g_send, g_recv = more
        block = out.at[at(c), quarter]
        return pltpu.make_async_remote_copy(
            src_ref=block,
            dst_ref=block,
            send_sem=g_send.at[way, c],
            recv_sem=g_recv.at[way, c],
            device_id=(me_d, far if way == 0 else sib),
            device_id_type=MESH,
        )

    for half in (0, 1):
        for c in range(chunks):
            to_sib(half, c).start()

    def add_far(c, _):
        to_sib(0, c).wait_recv()
        mine = part[at(c), far].astype(jnp.float32) + sib_in[0, at(c)].astype(jnp.float32)
        acc[at(c)] = mine.astype(acc.dtype)
        to_far(c).start()
        return 0

    lax.fori_loop(0, chunks, add_far, 0)
    own.wait()

    def settle(c, _):
        to_sib(1, c).wait_recv()
        to_far(c).wait_recv()
        total = (
            part[at(c), me_m].astype(jnp.float32)
            + sib_in[1, at(c)].astype(jnp.float32)
            + far_in[at(c)].astype(jnp.float32)
            + res[at(c)].astype(jnp.float32)
        )
        center = total - jnp.mean(total, axis=-1, keepdims=True)
        spread_sq = jnp.mean(center * center, axis=-1, keepdims=True)
        normed = center * lax.rsqrt(spread_sq + 1e-05) * gain[...] + shift[...]
        if gather:
            out[at(c), me_m] = normed.astype(out.dtype)
            spread(0, c, me_m).start()
            spread(1, c, me_m).start()
        else:
            out[at(c)] = normed.astype(out.dtype)
        return 0

    lax.fori_loop(0, chunks, settle, 0)
    if gather:

        def pass_on(c, _):
            spread(0, c, far).wait_recv()
            spread(2, c, far).start()
            return 0

        lax.fori_loop(0, chunks, pass_on, 0)
        for c in range(chunks):
            spread(1, c, sib).wait_recv()
            spread(2, c, sib_far).wait_recv()
            for way, quarter in ((0, me_m), (1, me_m), (2, far)):
                spread(way, c, quarter).wait_send()
    for c in range(chunks):
        to_sib(0, c).wait_send()
        to_sib(1, c).wait_send()
        to_far(c).wait_send()


def reduce_norm(part, resid, gain, shift, gather, collective_id):
    pages, n_mp, rows, width = part.shape
    chunk = 2 if pages % 2 == 0 else 1
    chunks = pages // chunk
    quarter = (pages, rows, width)
    vmem = pl.BlockSpec(memory_space=pltpu.VMEM)
    sems = [(1,), (2, chunks), (2, chunks), (chunks,), (chunks,)]
    if gather:
        sems += [(3, chunks), (3, chunks)]
    return pl.pallas_call(
        functools.partial(reduce_kernel, n_mp, chunk, gather),
        out_shape=jax.ShapeDtypeStruct(part.shape if gather else quarter, part.dtype),
        in_specs=[vmem, pl.BlockSpec(memory_space=pl.ANY), vmem, vmem],
        out_specs=vmem,
        scratch_shapes=[
            pltpu.VMEM((2, *quarter), part.dtype),
            pltpu.VMEM(quarter, part.dtype),
            pltpu.VMEM(quarter, part.dtype),
            pltpu.VMEM(quarter, part.dtype),
        ]
        + [pltpu.SemaphoreType.DMA(s) for s in sems],
        compiler_params=pltpu.CompilerParams(
            collective_id=collective_id, has_side_effects=True, vmem_limit_bytes=VMEM_BYTES
        ),
        name=f"reduce_{collective_id}",
    )(part, resid, gain.reshape(1, 1, width), shift.reshape(1, 1, width))


def pick_kernel(rows_ref, src, out):
    out[...] = src[...]


def pick(table, source, part=None):
    count = table.shape[0]
    if part is None:
        block = (1, *source.shape[1:])
        tail = (0,) * (source.ndim - 1)
        index = lambda i, t: (t[i], *tail)
        out_block, out_index = block, lambda i, t: (i, *tail)
        scalars = table
    else:
        block = (1, 1, *source.shape[2:])
        index = lambda i, t: (t[i], t[count], 0, 0)
        out_block, out_index = block, lambda i, t: (i, 0, 0, 0)
        scalars = jnp.concatenate([table, part.reshape(1)])
    return pl.pallas_call(
        pick_kernel,
        out_shape=jax.ShapeDtypeStruct((count, *out_block[1:]), source.dtype),
        grid_spec=pltpu.PrefetchScalarGridSpec(
            num_scalar_prefetch=1,
            grid=(count,),
            in_specs=[pl.BlockSpec(block, index)],
            out_specs=pl.BlockSpec(out_block, out_index),
        ),
        name="pick",
    )(scalars, source)


def project_kernel(rows_ref, src, weight, dealt, query, keys, values):
    page = src[0]
    dealt[0] = page
    width = query.shape[1]
    both = jnp.dot(page, weight[:, : 3 * width], preferred_element_type=jnp.float32)
    query[...] = both[:, :width].astype(query.dtype)
    keys[...] = both[:, width : 2 * width].astype(keys.dtype)
    values[...] = both[:, 2 * width :].astype(values.dtype)


def project(source_row, got, weight):
    count = source_row.shape[0]
    _, page, width = got.shape
    cols = weight.shape[1] // 4
    flat = jax.ShapeDtypeStruct((count * page, cols), got.dtype)
    flat_spec = pl.BlockSpec((page, cols), lambda i, t: (i, 0))
    return pl.pallas_call(
        project_kernel,
        out_shape=[jax.ShapeDtypeStruct((count, page, width), got.dtype), flat, flat, flat],
        grid_spec=pltpu.PrefetchScalarGridSpec(
            num_scalar_prefetch=1,
            grid=(count,),
            in_specs=[
                pl.BlockSpec((1, page, width), lambda i, t: (t[i], 0, 0)),
                pl.BlockSpec(weight.shape, lambda i, t: (0, 0)),
            ],
            out_specs=[
                pl.BlockSpec((1, page, width), lambda i, t: (i, 0, 0)),
                flat_spec,
                flat_spec,
                flat_spec,
            ],
        ),
        compiler_params=pltpu.CompilerParams(vmem_limit_bytes=VMEM_BYTES),
        name="project",
    )(source_row, got, weight)


def attend_kernel(query, keys, values, row_ids, col_ids, weight, out):
    width = query.shape[1]
    lane = lax.broadcasted_iota(jnp.int32, (1, width), 1)
    same = row_ids[...] == col_ids[...]
    rows = query[...].astype(jnp.float32) * HEAD**-0.5
    context = jnp.zeros(query.shape, jnp.float32)
    for head in range(width // HEAD):
        here = (lane >= head * HEAD) & (lane < (head + 1) * HEAD)
        picked = jnp.where(here, rows, 0.0).astype(query.dtype)
        scores = lax.dot_general(
            picked, keys[...], (((1,), (1,)), ((), ())), preferred_element_type=jnp.float32
        )
        scores = jnp.where(same, scores, -1e30)
        raised = jnp.exp(scores - jnp.max(scores, axis=1, keepdims=True))
        total = jnp.sum(raised, axis=1, keepdims=True)
        mixed = jnp.dot(
            raised.astype(values.dtype), values[...], preferred_element_type=jnp.float32
        )
        context = jnp.where(here, mixed / total, context)
    out[...] = lax.dot_general(
        context.astype(query.dtype),
        weight[...],
        (((1,), (1,)), ((), ())),
        preferred_element_type=jnp.float32,
    ).astype(out.dtype)


def attend(query, keys, values, ids, weight):
    tokens, width = query.shape
    block = 256 if tokens % 256 == 0 else 128
    whole = pl.BlockSpec((tokens, width), lambda i: (0, 0))
    features = weight.shape[0]
    return pl.pallas_call(
        attend_kernel,
        out_shape=jax.ShapeDtypeStruct((tokens, features), query.dtype),
        grid=(tokens // block,),
        in_specs=[
            pl.BlockSpec((block, width), lambda i: (i, 0)),
            whole,
            whole,
            pl.BlockSpec((block, 1), lambda i: (i, 0)),
            pl.BlockSpec((1, tokens), lambda i: (0, 0)),
            pl.BlockSpec((features, width), lambda i: (0, 3)),
        ],
        out_specs=pl.BlockSpec((block, features), lambda i: (i, 0)),
        compiler_params=pltpu.CompilerParams(vmem_limit_bytes=VMEM_BYTES),
        name="attend",
    )(query, keys, values, ids.reshape(tokens, 1), ids.reshape(1, tokens), weight)


def body(
    tokens,
    segment_ids,
    page_table,
    w_query,
    w_key,
    w_value,
    w_out,
    w_up,
    w_down,
    gain_first,
    shift_first,
    gain_second,
    shift_second,
):
    n_data, n_mp = lax.axis_size("dp"), lax.axis_size("mp")
    me_m = lax.axis_index("mp").astype(jnp.int32)
    pages_dev = page_table.shape[0]
    page = tokens.shape[0] // pages_dev
    width = tokens.shape[1]
    rows = page // n_mp
    slots_per = (pages_dev + n_data - 1) // n_data
    buffer_rows = n_data * slots_per
    target = page_table // pages_dev
    local_slot = page_table % pages_dev
    order = jnp.arange(pages_dev, dtype=jnp.int32)
    earlier = (target[:, None] == target[None, :]) & (order[:, None] < order[None, :])
    rank = jnp.sum(earlier.astype(jnp.int32), axis=0)
    position = target * slots_per + rank
    places = jnp.arange(buffer_rows, dtype=jnp.int32)
    placed = position[None, :] == places[:, None]
    page_of = jnp.sum(jnp.where(placed, order[None, :], 0), axis=1)
    ids_paged = segment_ids.reshape(pages_dev, page)
    send_ids = jnp.sum(jnp.where(placed[:, :, None], ids_paged[None], 0), axis=1)
    send_slots = jnp.sum(jnp.where(placed, local_slot[None, :] + 1, 0), axis=1) - 1
    meta = jnp.concatenate(
        [
            send_ids[:, None, :],
            jnp.broadcast_to(send_slots[:, None, None], (buffer_rows, 7, page)),
        ],
        axis=1,
    ).reshape(n_data, slots_per, 8, page)
    weight = jnp.concatenate([w_query, w_key, w_value, w_out.T], axis=1)
    send = pick(page_of, tokens.reshape(pages_dev, n_mp, rows, width), me_m)
    got, got_meta, full = swap(
        send.reshape(n_data, slots_per, rows, width), n_mp, 1, meta, weight
    )
    full_up = lax.all_gather(w_up, "dp", axis=0, tiled=True)
    full_down = lax.all_gather(w_down, "dp", axis=1, tiled=True)
    full = full.reshape(width, weight.shape[1])
    got_meta = got_meta.reshape(buffer_rows, 8, page)
    got_slots = got_meta[:, 1, 0]
    matches = got_slots[None, :] == order[:, None]
    source_row = jnp.sum(jnp.where(matches, places[None, :], 0), axis=1)
    dealt_ids = jnp.sum(jnp.where(matches[:, :, None], got_meta[None, :, 0, :], 0), axis=1)
    dealt, query, keys, values = project(source_row, got.reshape(buffer_rows, page, width), full)
    term = attend(query, keys, values, dealt_ids.reshape(-1), full)
    split = (pages_dev, n_mp, rows, width)
    first = reduce_norm(term.reshape(split), dealt.reshape(split), gain_first, shift_first, True, 2)
    hidden = jax.nn.gelu(
        jnp.dot(
            first.reshape(pages_dev * page, width), full_up, preferred_element_type=jnp.float32
        ),
        approximate=False,
    ).astype(jnp.bfloat16)
    fed = jnp.dot(hidden, full_down, preferred_element_type=jnp.float32).astype(jnp.bfloat16)
    second = reduce_norm(fed.reshape(split), first, gain_second, shift_second, False, 3)
    back = pick(jnp.maximum(got_slots, 0), second)
    [returned] = swap(back.reshape(n_data, slots_per, rows, width), n_mp, 4)
    mixed = pick(position, returned.reshape(buffer_rows, page, width))
    kv_cache = jnp.stack([keys, values], axis=1)
    return (mixed.reshape(pages_dev * page, width), kv_cache)


def solution(mesh):
    return jax.shard_map(
        body,
        mesh=mesh,
        in_specs=(
            P("dp", None),
            P("dp"),
            P("dp"),
            P("dp", "mp"),
            P("dp", "mp"),
            P("dp", "mp"),
            P("mp", "dp"),
            P("dp", "mp"),
            P("mp", "dp"),
            P(),
            P(),
            P(),
            P(),
        ),
        out_specs=(P("dp", None), P("dp", None, "mp")),
        check_vma=False,
    )
```

```python
import functools

import jax
import jax.numpy as jnp
from jax import lax
from jax.experimental import pallas as pl
from jax.experimental.pallas import tpu as pltpu
from jax.sharding import PartitionSpec as P

HEAD = 64
MESH = pl.DeviceIdType.MESH
VMEM_BYTES = 48 * 1024 * 1024


def mp_peers(me_m, n_mp):
    return me_m + 1 - 2 * lax.rem(me_m, 2), lax.rem(me_m + 2, n_mp)


def swap_kernel(n_dp, n_mp, with_extra, *refs):
    if with_extra:
        send, meta, weight, recv, got_meta, full, *sems = refs
    else:
        send, recv, *sems = refs
    local, a_send, a_recv, f_send, f_recv, *more = sems
    me_d, me_m = lax.axis_index("dp"), lax.axis_index("mp")
    sib, far = mp_peers(me_m, n_mp)
    barrier = pltpu.get_barrier_semaphore()
    for k in range(1, n_dp):
        pl.semaphore_signal(
            barrier, inc=1, device_id=(lax.rem(me_d + k, n_dp), me_m), device_id_type=MESH
        )
    for peer in (sib, far):
        pl.semaphore_signal(barrier, inc=1, device_id=(me_d, peer), device_id_type=MESH)
    pl.semaphore_wait(barrier, n_dp + 1)

    def remote(src, dst, s_sem, r_sem, dev):
        return pltpu.make_async_remote_copy(
            src_ref=src,
            dst_ref=dst,
            send_sem=s_sem,
            recv_sem=r_sem,
            device_id=dev,
            device_id_type=MESH,
        )

    def source(k):
        return lax.rem(me_d - k + n_dp, n_dp)

    own = pltpu.make_async_copy(send.at[me_d], recv.at[me_d, :, me_m], local.at[0])
    own.start()
    outs = []
    if with_extra:
        m_send, m_recv, z_send, z_recv, y_send, y_recv = more
        own_meta = pltpu.make_async_copy(meta.at[me_d], got_meta.at[me_d], local.at[1])
        own_meta.start()
        own_w = pltpu.make_async_copy(weight, full.at[me_d], local.at[2])
        own_w.start()
        for k in range(1, n_dp):
            to = lax.rem(me_d + k, n_dp)
            outs.append(
                remote(meta.at[to], got_meta.at[me_d], m_send.at[k], m_recv.at[k], (to, me_m))
            )
            outs[-1].start()
    slots = send.shape[1]
    for slot in range(slots):
        for k in range(1, n_dp):
            to = lax.rem(me_d + k, n_dp)
            outs.append(
                remote(
                    send.at[to, slot],
                    recv.at[me_d, slot, me_m],
                    a_send.at[slot, k],
                    a_recv.at[slot, k],
                    (to, me_m),
                )
            )
            outs[-1].start()
    if with_extra:
        rows = n_dp // 2
        b = lax.rem(me_d, 2)
        a = (me_d - b) // 2
        across = me_d + 1 - 2 * b
        outs.append(remote(weight, full.at[me_d], y_send.at[0], y_recv.at[0], (me_d + 1 - 2 * b, me_m)))
        outs[-1].start()
        for k in range(1, rows):
            to = lax.rem(a + k, rows) * 2 + b
            outs.append(remote(weight, full.at[me_d], z_send.at[k], z_recv.at[k], (to, me_m)))
            outs[-1].start()

    def copy_on(way, slot, k, quarter):
        block = recv.at[source(k), slot, quarter]
        peer = far if way == 0 else sib
        return remote(
            block, block, f_send.at[way, slot, k], f_recv.at[way, slot, k], (me_d, peer)
        )

    def hand_on(slot, k):
        for way in (0, 1):
            outs.append(copy_on(way, slot, k, me_m))
            outs[-1].start()

    def hand_far(slot, k):
        copy_on(0, slot, k, far).wait_recv()
        outs.append(copy_on(2, slot, k, far))
        outs[-1].start()

    own.wait()
    for slot in range(slots):
        hand_on(slot, 0)
    for slot in range(slots):
        for k in range(1, n_dp):
            block = recv.at[source(k), slot, me_m]
            remote(block, block, a_send.at[slot, k], a_recv.at[slot, k], (me_d, far)).wait_recv()
            hand_on(slot, k)
            hand_far(slot, k - 1)
        hand_far(slot, n_dp - 1)
    if with_extra:
        for k in range(1, rows):
            block = full.at[lax.rem(a - k + rows, rows) * 2 + b]
            remote(block, block, z_send.at[k], z_recv.at[k], (across, me_m)).wait_recv()
            outs.append(remote(block, block, y_send.at[k], y_recv.at[k], (across, me_m)))
            outs[-1].start()
        for k in range(rows):
            block = full.at[lax.rem(a - k + rows, rows) * 2 + 1 - b]
            remote(block, block, y_send.at[k], y_recv.at[k], (across, me_m)).wait_recv()
        for k in range(1, n_dp):
            block = got_meta.at[source(k)]
            remote(block, block, m_send.at[k], m_recv.at[k], (across, me_m)).wait_recv()
        own_meta.wait()
        own_w.wait()
    sib_far = lax.rem(sib + 2, n_mp)
    for slot in range(slots):
        for k in range(n_dp):
            copy_on(1, slot, k, sib).wait_recv()
            copy_on(2, slot, k, sib_far).wait_recv()
    for copy in outs:
        copy.wait_send()


def swap(send, n_mp, collective_id, meta=None, weight=None):
    n_dp, slots, rows, width = send.shape
    with_extra = meta is not None
    any_spec = pl.BlockSpec(memory_space=pl.ANY)
    outs = [jax.ShapeDtypeStruct((n_dp, slots, n_mp, rows, width), send.dtype)]
    sems = [(3,)] + [(slots, n_dp)] * 2 + [(3, slots, n_dp)] * 2
    args = [send]
    if with_extra:
        outs += [
            jax.ShapeDtypeStruct(meta.shape, meta.dtype),
            jax.ShapeDtypeStruct((n_dp, *weight.shape), weight.dtype),
        ]
        sems += [(n_dp,), (n_dp,)] + [(n_dp // 2,)] * 4
        args += [meta, weight]
    return pl.pallas_call(
        functools.partial(swap_kernel, n_dp, n_mp, with_extra),
        out_shape=outs,
        in_specs=[any_spec] * len(args),
        out_specs=[any_spec] * len(outs),
        scratch_shapes=[pltpu.SemaphoreType.DMA(s) for s in sems],
        compiler_params=pltpu.CompilerParams(collective_id=collective_id, has_side_effects=True),
        name=f"swap_{collective_id}",
    )(*args)


def pick_kernel(count, part, table, src, out, sem):
    copies = []
    for i in range(count):
        block = src.at[table[i]]
        if part:
            block = block.at[table[count]]
        copies.append(pltpu.make_async_copy(block, out.at[i], sem.at[i]))
        copies[-1].start()
    for copy in copies:
        copy.wait()


def pick(table, source, part=None):
    count = table.shape[0]
    shape = source.shape[1:] if part is None else source.shape[2:]
    scalars = table if part is None else jnp.concatenate([table, part.reshape(1)])
    any_spec = pl.BlockSpec(memory_space=pl.ANY)
    return pl.pallas_call(
        functools.partial(pick_kernel, count, part is not None),
        out_shape=jax.ShapeDtypeStruct((count, *shape), source.dtype),
        in_specs=[pl.BlockSpec(memory_space=pltpu.SMEM), any_spec],
        out_specs=any_spec,
        scratch_shapes=[pltpu.SemaphoreType.DMA((count,))],
        name="pick",
    )(scalars, source)


def project_kernel(table, src, weight, dealt, query, keys, values, pages, w_held, sem):
    count, page, width = pages.shape
    cols = query.shape[1]
    n_mp, rows = src.shape[1], src.shape[2]
    w_copy = pltpu.make_async_copy(weight, w_held, sem.at[2 * count])
    w_copy.start()
    copies, quarters = [], []
    for i in range(count):
        block = src.at[table[i]]
        copies.append(
            pltpu.make_async_copy(block, pages.at[i].reshape(n_mp, rows, width), sem.at[i])
        )
        copies[-1].start()
        quarters.append(
            pltpu.make_async_copy(block.at[table[count]], dealt.at[i], sem.at[count + i])
        )
        quarters[-1].start()
    w_copy.wait()
    group = 2 if count % 2 == 0 else 1
    for i in range(0, count, group):
        for k in range(group):
            copies[i + k].wait()
        held = pages[i : i + group].reshape(group * page, width)
        both = jnp.dot(held, w_held[:, : 3 * cols], preferred_element_type=jnp.float32)
        at = pl.ds(i * page, group * page)
        query[at] = both[:, :cols].astype(query.dtype)
        keys[at] = both[:, cols : 2 * cols].astype(keys.dtype)
        values[at] = both[:, 2 * cols :].astype(values.dtype)
    for copy in quarters:
        copy.wait()


def project(source_row, me_m, got, weight):
    count = source_row.shape[0]
    _, n_mp, rows, width = got.shape
    page = n_mp * rows
    cols = weight.shape[1] // 4
    flat = jax.ShapeDtypeStruct((count * page, cols), got.dtype)
    any_spec = pl.BlockSpec(memory_space=pl.ANY)
    vmem = pl.BlockSpec(memory_space=pltpu.VMEM)
    return pl.pallas_call(
        project_kernel,
        out_shape=[jax.ShapeDtypeStruct((count, rows, width), got.dtype), flat, flat, flat],
        in_specs=[pl.BlockSpec(memory_space=pltpu.SMEM), any_spec, any_spec],
        out_specs=[any_spec, vmem, vmem, vmem],
        scratch_shapes=[
            pltpu.VMEM((count, page, width), got.dtype),
            pltpu.VMEM(weight.shape, weight.dtype),
            pltpu.SemaphoreType.DMA((2 * count + 1,)),
        ],
        compiler_params=pltpu.CompilerParams(vmem_limit_bytes=VMEM_BYTES),
        name="project",
    )(jnp.concatenate([source_row, me_m.reshape(1)]), got, weight)


def attend_rows(at, query, keys, values, row_ids, col_ids, weight):
    width = query.shape[1]
    lane = lax.broadcasted_iota(jnp.int32, (1, width), 1)
    same = row_ids[at] == col_ids[...]
    rows = query[at].astype(jnp.float32) * HEAD**-0.5
    context = jnp.zeros(rows.shape, jnp.float32)
    for head in range(width // HEAD):
        here = (lane >= head * HEAD) & (lane < (head + 1) * HEAD)
        picked = jnp.where(here, rows, 0.0).astype(query.dtype)
        scores = lax.dot_general(
            picked, keys[...], (((1,), (1,)), ((), ())), preferred_element_type=jnp.float32
        )
        scores = jnp.where(same, scores, -1e30)
        raised = jnp.exp(scores - jnp.max(scores, axis=1, keepdims=True))
        total = jnp.sum(raised, axis=1, keepdims=True)
        mixed = jnp.dot(
            raised.astype(values.dtype), values[...], preferred_element_type=jnp.float32
        )
        context = jnp.where(here, mixed / total, context)
    return lax.dot_general(
        context.astype(query.dtype),
        weight[...],
        (((1,), (1,)), ((), ())),
        preferred_element_type=jnp.float32,
    )


def feed_rows(chunk, first, w_up, w_down):
    pages, n_mp, rows, width = first.shape
    raised = jnp.dot(
        first[chunk].reshape(-1, width), w_up[...], preferred_element_type=jnp.float32
    )
    hidden = 0.5 * raised * (1.0 + lax.erf(raised * 0.5**0.5))
    return jnp.dot(hidden.astype(first.dtype), w_down[...], preferred_element_type=jnp.float32)


def reduce_kernel(n_mp, chunk, gather, *refs):
    n_work = 6 if gather else 3
    work, refs = refs[:n_work], refs[n_work:]
    resid, gain, shift, out, part, sib_in, acc, far_in, res, *sems = refs
    local, s_send, s_recv, x_send, x_recv, *more = sems
    me_d, me_m = lax.axis_index("dp"), lax.axis_index("mp")
    sib, far = mp_peers(me_m, n_mp)
    sib_far = lax.rem(sib + 2, n_mp)
    chunks = part.shape[0] // chunk
    barrier = pltpu.get_barrier_semaphore()
    for peer in (sib, far):
        pl.semaphore_signal(barrier, inc=1, device_id=(me_d, peer), device_id_type=MESH)
    pl.semaphore_wait(barrier, 2)
    own = pltpu.make_async_copy(resid if gather else resid.at[:, me_m], res, local.at[0])
    own.start()

    def at(c):
        return pl.ds(c * chunk, chunk)

    def to_sib(half, c):
        quarter = sib_far if half == 0 else sib
        return pltpu.make_async_remote_copy(
            src_ref=part.at[at(c), quarter],
            dst_ref=sib_in.at[half, at(c)],
            send_sem=s_send.at[half, c],
            recv_sem=s_recv.at[half, c],
            device_id=(me_d, sib),
            device_id_type=MESH,
        )

    def to_far(c):
        return pltpu.make_async_remote_copy(
            src_ref=acc.at[at(c)],
            dst_ref=far_in.at[at(c)],
            send_sem=x_send.at[c],
            recv_sem=x_recv.at[c],
            device_id=(me_d, far),
            device_id_type=MESH,
        )

    def spread(way, c, quarter):
        g_send, g_recv = more
        block = out.at[at(c), quarter]
        return pltpu.make_async_remote_copy(
            src_ref=block,
            dst_ref=block,
            send_sem=g_send.at[way, c],
            recv_sem=g_recv.at[way, c],
            device_id=(me_d, far if way == 0 else sib),
            device_id_type=MESH,
        )

    def produce(c):
        if gather:
            tall = chunk * part.shape[1] * part.shape[2]
            made = attend_rows(pl.ds(pl.multiple_of(c * tall, tall), tall), *work)
        else:
            made = feed_rows(at(c), *work)
        part[at(c)] = made.astype(part.dtype).reshape(chunk, *part.shape[1:])
        to_sib(0, c).start()
        to_sib(1, c).start()

    def add_far(c):
        to_sib(0, c).wait_recv()
        mine = part[at(c), far].astype(jnp.float32) + sib_in[0, at(c)].astype(jnp.float32)
        acc[at(c)] = mine.astype(acc.dtype)
        to_far(c).start()

    def settle(c):
        to_sib(1, c).wait_recv()
        to_far(c).wait_recv()
        total = (
            part[at(c), me_m].astype(jnp.float32)
            + sib_in[1, at(c)].astype(jnp.float32)
            + far_in[at(c)].astype(jnp.float32)
            + res[at(c)].astype(jnp.float32)
        )
        center = total - jnp.mean(total, axis=-1, keepdims=True)
        spread_sq = jnp.mean(center * center, axis=-1, keepdims=True)
        normed = center * lax.rsqrt(spread_sq + 1e-05) * gain[...] + shift[...]
        if gather:
            out[at(c), me_m] = normed.astype(out.dtype)
            spread(0, c, me_m).start()
            spread(1, c, me_m).start()
        else:
            out[at(c)] = normed.astype(out.dtype)

    produce(0)
    own.wait()

    def step(c, _):
        produce(c)
        add_far(c - 1)

        @pl.when(c >= 3)
        def _():
            settle(c - 3)

        return 0

    lax.fori_loop(1, chunks, step, 0)
    add_far(chunks - 1)
    for c in range(max(chunks - 3, 0), chunks):
        settle(c)
    if gather:

        def pass_on(c, _):
            spread(0, c, far).wait_recv()
            spread(2, c, far).start()
            return 0

        lax.fori_loop(0, chunks, pass_on, 0)
        for c in range(chunks):
            spread(1, c, sib).wait_recv()
            spread(2, c, sib_far).wait_recv()
            for way, quarter in ((0, me_m), (1, me_m), (2, far)):
                spread(way, c, quarter).wait_send()
    for c in range(chunks):
        to_sib(0, c).wait_send()
        to_sib(1, c).wait_send()
        to_far(c).wait_send()


def reduce_norm(work, split, resid, gain, shift, gather, collective_id):
    pages, n_mp, rows, width = split
    chunk = 2 if pages % 2 == 0 else 1
    chunks = pages // chunk
    quarter = (pages, rows, width)
    dtype = resid.dtype
    vmem = pl.BlockSpec(memory_space=pltpu.VMEM)
    out_shape = split if gather else quarter
    sems = [(1,), (2, chunks), (2, chunks), (chunks,), (chunks,)]
    if gather:
        sems += [(3, chunks), (3, chunks)]
    return pl.pallas_call(
        functools.partial(reduce_kernel, n_mp, chunk, gather),
        out_shape=jax.ShapeDtypeStruct(out_shape, dtype),
        in_specs=[vmem] * len(work) + [pl.BlockSpec(memory_space=pl.ANY), vmem, vmem],
        out_specs=vmem,
        scratch_shapes=[
            pltpu.VMEM(split, dtype),
            pltpu.VMEM((2, *quarter), dtype),
            pltpu.VMEM(quarter, dtype),
            pltpu.VMEM(quarter, dtype),
            pltpu.VMEM(quarter, dtype),
        ]
        + [pltpu.SemaphoreType.DMA(s) for s in sems],
        compiler_params=pltpu.CompilerParams(
            collective_id=collective_id, has_side_effects=True, vmem_limit_bytes=VMEM_BYTES
        ),
        name=f"reduce_{collective_id}",
    )(*work, resid, gain.reshape(1, 1, width), shift.reshape(1, 1, width))


def body(
    tokens,
    segment_ids,
    page_table,
    w_query,
    w_key,
    w_value,
    w_out,
    w_up,
    w_down,
    gain_first,
    shift_first,
    gain_second,
    shift_second,
):
    n_data, n_mp = lax.axis_size("dp"), lax.axis_size("mp")
    me_m = lax.axis_index("mp").astype(jnp.int32)
    pages_dev = page_table.shape[0]
    page = tokens.shape[0] // pages_dev
    width = tokens.shape[1]
    rows = page // n_mp
    slots_per = (pages_dev + n_data - 1) // n_data
    buffer_rows = n_data * slots_per
    target = page_table // pages_dev
    local_slot = page_table % pages_dev
    order = jnp.arange(pages_dev, dtype=jnp.int32)
    earlier = (target[:, None] == target[None, :]) & (order[:, None] < order[None, :])
    rank = jnp.sum(earlier.astype(jnp.int32), axis=0)
    position = target * slots_per + rank
    places = jnp.arange(buffer_rows, dtype=jnp.int32)
    placed = position[None, :] == places[:, None]
    page_of = jnp.sum(jnp.where(placed, order[None, :], 0), axis=1)
    ids_paged = segment_ids.reshape(pages_dev, page)
    send_ids = jnp.sum(jnp.where(placed[:, :, None], ids_paged[None], 0), axis=1)
    send_slots = jnp.sum(jnp.where(placed, local_slot[None, :] + 1, 0), axis=1) - 1
    meta = jnp.concatenate(
        [
            send_ids[:, None, :],
            jnp.broadcast_to(send_slots[:, None, None], (buffer_rows, 7, page)),
        ],
        axis=1,
    ).reshape(n_data, slots_per, 8, page)
    weight = jnp.concatenate([w_query, w_key, w_value, w_out.T], axis=1)
    send = pick(page_of, tokens.reshape(pages_dev, n_mp, rows, width), me_m)
    got, got_meta, full = swap(
        send.reshape(n_data, slots_per, rows, width), n_mp, 1, meta, weight
    )
    w_up, w_down, got_meta = lax.optimization_barrier((w_up, w_down, got_meta))
    full_up = lax.all_gather(w_up, "dp", axis=0, tiled=True)
    full_down = lax.all_gather(w_down, "dp", axis=1, tiled=True)
    full = full.reshape(width, weight.shape[1])
    got_meta = got_meta.reshape(buffer_rows, 8, page)
    got_slots = got_meta[:, 1, 0]
    matches = got_slots[None, :] == order[:, None]
    source_row = jnp.sum(jnp.where(matches, places[None, :], 0), axis=1)
    dealt_ids = jnp.sum(jnp.where(matches[:, :, None], got_meta[None, :, 0, :], 0), axis=1)
    dealt, query, keys, values = project(
        source_row, me_m, got.reshape(buffer_rows, n_mp, rows, width), full
    )
    split = (pages_dev, n_mp, rows, width)
    ids = dealt_ids.reshape(-1)
    attending = (query, keys, values, ids.reshape(-1, 1), ids.reshape(1, -1), full[:, -query.shape[1] :])
    first = reduce_norm(attending, split, dealt, gain_first, shift_first, True, 2)
    feeding = (first, full_up, full_down)
    second = reduce_norm(feeding, split, first, gain_second, shift_second, False, 3)
    back = pick(jnp.maximum(got_slots, 0), second)
    [returned] = swap(back.reshape(n_data, slots_per, rows, width), n_mp, 4)
    mixed = pick(position, returned.reshape(buffer_rows, page, width))
    kv_cache = jnp.stack([keys, values], axis=1)
    return (mixed.reshape(pages_dev * page, width), kv_cache)


def solution(mesh):
    return jax.shard_map(
        body,
        mesh=mesh,
        in_specs=(
            P("dp", None),
            P("dp"),
            P("dp"),
            P("dp", "mp"),
            P("dp", "mp"),
            P("dp", "mp"),
            P("mp", "dp"),
            P("dp", "mp"),
            P("mp", "dp"),
            P(),
            P(),
            P(),
            P(),
        ),
        out_specs=(P("dp", None), P("dp", None, "mp")),
        check_vma=False,
    )
```
